128 devices in a mesh: chan: 32 (over x, z, core), seg: 4 (over y).
Axes of the slice: x: 4, y: 4, z: 4, core: 2. Of those that a mesh axis runs over, the one named last changes fastest.
Arguments:
- traces: bfloat16 [8192, 8, 4096], P('chan', 'seg'), may hold values from -6 to 6
- pairs: int32 [128, 2], P('chan'), may hold values from 0 to 31, as said below
Outputs:
- stacked: float32 [4, 128, 256, 256], P('seg', 'chan')
The draws below stay inside these ranges and needn't reach their ends.
Inputs may be any that keep to these rules, and one draw needn't show every extreme that they name: `pairs`: the two blocks of a row differ. Row p stands on the device of block h = p // 4. Each block of the row lies within 4 blocks of h, or is the block (h + 16) mod 32, where the cable loops back; in every draw every device has a row with that looped block and a row reaching exactly 4, and block 0 and block 31 both appear.
All inputs are finite; a program needn't handle non-finite values.
Results may differ from the reference program's by a relative error of at most 0.0043.
Values may be sent and summed in bfloat16 or wider, within the bound.
A program may use at most 128 MiB of HBM per device.

```python
import math
import jax
import jax.numpy as jnp
from jax import lax

CB = 256
L = 4096
NF = 512
FLO = 64
HW = 64
LAGSTEP = 16
PAIR_DEV = 4
REACH = 4
BLOCKS = 32
CHANNELS = 8192
SEGMENTS = 8
NLAG = 4
PAIRS = 128


def draw_pairs(key, part):
    key = jax.random.fold_in(key, 11)
    key_near, key_step, key_loop = jax.random.split(key, 3)
    home_index = jnp.arange(PAIRS, dtype=jnp.int32) // PAIR_DEV
    slot_index = jnp.arange(PAIRS, dtype=jnp.int32) % PAIR_DEV
    near_offset = jax.random.randint(key_near, (PAIRS,), -1, 2, dtype=jnp.int32)
    at_edge = (home_index == 0) | (home_index == BLOCKS - 1)
    near_offset = jnp.where(at_edge, 0, near_offset)
    near_first = jnp.clip(home_index + near_offset, 0, BLOCKS - 1)
    step_size = jax.random.randint(key_step, (PAIRS,), 1, 4, dtype=jnp.int32)
    near_second = jnp.where(near_first + step_size <= BLOCKS - 1, near_first + step_size, near_first - step_size)
    reach_second = jnp.where(home_index + REACH <= BLOCKS - 1, home_index + REACH, home_index - REACH)
    is_reach = slot_index == 0
    near_first = jnp.where(is_reach, home_index, near_first)
    near_second = jnp.where(is_reach, reach_second, near_second)
    loop_first = (home_index + BLOCKS // 2) % BLOCKS
    loop_offset = jax.random.randint(key_loop, (PAIRS,), 1 - REACH, REACH, dtype=jnp.int32)
    loop_second = jnp.clip(home_index + loop_offset, 0, BLOCKS - 1)
    is_loop = slot_index == PAIR_DEV - 1
    first_block = jnp.where(is_loop, loop_first, near_first)
    second_block = jnp.where(is_loop, loop_second, near_second)
    return jnp.stack([first_block, second_block], axis=1).astype(jnp.int32)


def level_of(key, dims, cuts, low, largest):
    def one(axis_at, blocks):
        draws = jax.random.uniform(jax.random.fold_in(jax.random.fold_in(key, 6), axis_at), (blocks,), jnp.float32, low / len(cuts), largest / len(cuts))
        return jnp.repeat(jnp.exp(draws), dims[axis_at] // blocks).reshape((-1,) + (1,) * (len(dims) - axis_at - 1))

    factor_of = one(*cuts[0])
    for cut in cuts[1:]:
        factor_of = factor_of * one(*cut)
    return factor_of


def normal_values(key, shape, width, limit, cuts=(), held_as=jnp.bfloat16):
    entries = jax.random.normal(key, shape, jnp.float32) * width
    if len(cuts) > 0:
        entries = level_of(key, shape, cuts, -0.22, 0.18) * entries
    return jnp.clip(entries, min=-limit, max=limit).astype(held_as)


def setup_inputs(seed: int = 0) -> dict:
    keys = jax.random.split(jax.random.key(seed), 3)
    return {
        "traces": normal_values(keys[0], (CHANNELS, SEGMENTS, L), 1.0, 6.0, ((0, 32), (1, 4))),
        "pairs": draw_pairs(jax.random.fold_in(keys[2], 71), 0),
    }


def build_tables(length, bins, lowest):
    sample_index = jnp.arange(length, dtype=jnp.int32)
    bin_index = lowest + jnp.arange(bins, dtype=jnp.int32)
    turn_count = sample_index[:, None] * bin_index[None, :] % length
    angles = 2.0 * math.pi / length * turn_count.astype(jnp.float32)
    window_taper = 0.5 - 0.5 * jnp.cos(2.0 * math.pi / length * sample_index.astype(jnp.float32))
    normal_scale = 1.0 / math.sqrt(length)
    cosine = window_taper[:, None] * jnp.cos(angles) * normal_scale
    sine_part = -window_taper[:, None] * jnp.sin(angles) * normal_scale
    dft_table = jnp.concatenate([cosine, sine_part], axis=1).astype(jnp.bfloat16)
    bin_rows = jnp.arange(bins, dtype=jnp.int32)
    in_window = (jnp.abs(bin_rows[:, None] - bin_rows[None, :]) <= HW).astype(jnp.float32)
    counts = lax.optimization_barrier(jnp.sum(in_window, axis=0))
    matrix = in_window / counts[None, :]
    return (dft_table, matrix)

def whiten(traces_block, dft_table, matrix):
    chan_block, seg_local, length = traces_block.shape
    row_block = traces_block.reshape(chan_block * seg_local, length)
    spectrum = jnp.dot(row_block, dft_table, preferred_element_type=jnp.float32)
    real_part = spectrum[:, :NF]
    imag_part = spectrum[:, NF:]
    power_spec = real_part * real_part + imag_part * imag_part
    smoothed = jnp.dot(power_spec, matrix, precision=lax.Precision.HIGHEST)
    factor = 1.0 / jnp.sqrt(smoothed + 1e-06)
    whitened = jnp.concatenate([real_part * factor, imag_part * factor], axis=1).astype(jnp.bfloat16)
    return whitened.reshape(chan_block, seg_local, 2 * NF)

def phases(lag_shifts, length):
    bin_index = FLO + jnp.arange(NF, dtype=jnp.int32)
    turn_count = lag_shifts[:, None] * bin_index[None, :] % length
    angles = 2.0 * math.pi / length * turn_count.astype(jnp.float32)
    return (jnp.cos(angles), jnp.sin(angles))

def rotate(spectra, cosine, sine_part):
    shape_out = (cosine.shape[0],) + (1,) * (spectra.ndim - 1) + (NF,)
    cosine = cosine.reshape(shape_out)
    sine_part = sine_part.reshape(shape_out)
    real_part = spectra[..., :NF].astype(jnp.float32)[None]
    imag_part = spectra[..., NF:].astype(jnp.float32)[None]
    real_rot = real_part * cosine - imag_part * sine_part
    imag_rot = real_part * sine_part + imag_part * cosine
    return jnp.concatenate([real_rot, imag_rot], axis=-1).astype(jnp.bfloat16)

def reference(traces, pairs):
    dft_table, matrix = build_tables(L, NF, FLO)
    blocks = traces.reshape(BLOCKS, CB, SEGMENTS, L)
    whitened = lax.map(lambda traces_block: whiten(traces_block, dft_table, matrix), blocks)
    lag_shifts = (jnp.arange(NLAG, dtype=jnp.int32) - NLAG // 2) * LAGSTEP
    cosine, sine_part = phases(lag_shifts, L)
    stack_scale = 1.0 / math.sqrt(NF * SEGMENTS)

    def one_pair(pair_row):
        first_spec = whitened[pair_row[0]]
        second_spec = whitened[pair_row[1]].reshape(CB, -1).astype(jnp.float32)
        rotated = rotate(first_spec, cosine, sine_part).reshape(NLAG, CB, -1).astype(jnp.float32)
        return jnp.einsum('kix,jx->kij', rotated, second_spec) * stack_scale
    stacked = lax.map(one_pair, pairs)
    return jnp.transpose(stacked, (1, 0, 2, 3))
```

```python
import math

import jax
import jax.numpy as jnp
import numpy as np
from jax import lax
from jax.experimental import pallas as pl
from jax.experimental.pallas import tpu as pltpu
from jax.sharding import PartitionSpec as P

CB = 256
L = 4096
NF = 512
FLO = 64
HW = 64
LAGSTEP = 16
NLAG = 4
PAIRS = 4
BLOCKS = 32
SEG = 2
CHUNK = 64
CHUNKS = CB // CHUNK
GROUPS = ((0, 1), (2,), (3,))
TABLE_CUTS = 4
MESH = pl.DeviceIdType.MESH
BF16 = jnp.bfloat16
F32 = jnp.float32

ZP, ZM, ZA, ZB, ZC, XN, XE, ZE, LA, LB, SB = 0, 2, 4, 5, 6, 7, 9, 10, 11, 15, 19
COPIES = 25


def host_tables():
    sample = np.arange(L)
    bins = FLO + np.arange(NF)
    angles = 2.0 * np.pi / L * ((sample[:, None] * bins[None, :]) % L)
    taper = (0.5 - 0.5 * np.cos(2.0 * np.pi / L * sample))[:, None] / math.sqrt(L)
    table = np.concatenate([taper * np.cos(angles), -taper * np.sin(angles)], axis=1)
    rows = np.arange(NF)
    window = np.abs(rows[:, None] - rows[None, :]) <= HW
    phase = 2.0 * np.pi / L * ((LAGSTEP * bins) % L)
    small = np.zeros((8, NF), np.float32)
    small[0], small[1] = np.cos(phase), np.sin(phase)
    small[2], small[3] = np.cos(2.0 * phase), np.sin(2.0 * phase)
    small[4] = 1.0 / window.sum(axis=0)
    return table.astype(BF16), window.astype(BF16), small


def regions(group):
    new = len(group) * CHUNK
    old = group[0] * CHUNK
    shapes = [(new, -(-(old + new) // 128) * 128)]
    if old:
        shapes.append((new, -(-old // 128) * 128))
    return new, old, shapes


def kernel(traces, table_hbm, window, small, pairs, out, *scratch):
    pools = scratch[:CHUNKS]
    scratch = scratch[CHUNKS:]
    spans = [len(regions(group)[2]) for group in GROUPS]
    sends, lands = [], []
    for span in spans:
        sends.append(scratch[:span])
        lands.append(scratch[span : 2 * span])
        scratch = scratch[2 * span :]
    rows_in, table, white, rot, in_sem, ssem, rsem, ysem, yrsem = scratch

    h = lax.axis_index("chan")
    y = lax.axis_index("seg")
    core = h % 2
    z = (h // 2) % 4
    x = h // 8
    away = 1 - 2 * (z // 2)
    outer = (z == 0) | (z == 3)
    gives = (x + away >= 0) & (x + away <= 3)
    takes = (x - away >= 0) & (x - away <= 3)

    def node(xx, zz, cc=None):
        return ((xx % 4) * 8 + (zz % 4) * 2 + (core if cc is None else cc), y)

    def slot(xx, zz, cc=None):
        return node(xx, zz, cc)[0]

    sibling = node(x, z, 1 - core)
    partners = [node(x, z + 1), node(x, z + 3), node(x + 1, z), node(x + 3, z), sibling]
    partners += [(h, (y + d) % 4) for d in (1, 2, 3)]

    fetch_rows = [
        pltpu.make_async_copy(
            traces.at[pl.ds(t * CHUNK, CHUNK)], rows_in.at[pl.ds(t * CHUNK, CHUNK)], in_sem.at[t]
        )
        for t in range(CHUNKS)
    ]
    cut = L // TABLE_CUTS
    fetch_table = [
        pltpu.make_async_copy(
            table_hbm.at[pl.ds(i * cut, cut)], table.at[pl.ds(i * cut, cut)], in_sem.at[CHUNKS + i]
        )
        for i in range(TABLE_CUTS)
    ]
    fetch_rows[0].start()
    for copy in fetch_table:
        copy.start()
    for copy in fetch_rows[1:]:
        copy.start()

    barrier = pltpu.get_barrier_semaphore()
    for partner in partners:
        pl.semaphore_signal(barrier, inc=1, device_id=partner, device_id_type=MESH)

    def spectra(t):
        fetch_rows[t].wait()
        rows = rows_in[t * CHUNK : (t + 1) * CHUNK].reshape(SEG * CHUNK, L)
        if t == 0:
            spec = jnp.zeros((SEG * CHUNK, 2 * NF), F32)
            for i in range(TABLE_CUTS):
                fetch_table[i].wait()
                spec += jnp.dot(
                    rows[:, i * cut : (i + 1) * cut],
                    table[i * cut : (i + 1) * cut],
                    preferred_element_type=F32,
                )
        else:
            spec = jnp.dot(rows, table[...], preferred_element_type=F32)
        real, imag = spec[:, :NF], spec[:, NF:]
        power = real * real + imag * imag
        high = power.astype(BF16)
        low = (power - high.astype(F32)).astype(BF16)
        smooth = jnp.dot(high, window[...], preferred_element_type=F32)
        smooth += jnp.dot(low, window[...], preferred_element_type=F32)
        factor = lax.rsqrt(smooth * small[4:5, :] + 1e-06)
        for j in range(2 * NF // 128):
            part = real if j * 128 < NF else imag
            lanes = slice(j * 128 % NF, j * 128 % NF + 128)
            white[j] = part[:, lanes] * factor[:, lanes]
            for s in range(SEG):
                rows = white[j, pl.ds(s, CHUNK, stride=SEG), :]
                pools[t][h, s, :, j * 128 : (j + 1) * 128] = rows.astype(BF16)

    started = []

    def remote(t, what, block, part, target):
        view = pools[t].at[(block, *part)]
        return pltpu.make_async_remote_copy(
            src_ref=view,
            dst_ref=view,
            send_sem=ssem.at[t, what],
            recv_sem=rsem.at[t, what],
            device_id=target,
            device_id_type=MESH,
        )

    def on(condition, act):
        if condition is None:
            act()
        else:
            pl.when(condition)(act)

    def send(t, what, block, part, target, condition=None):
        on(condition, lambda: remote(t, what, block, part, target).start())
        started.append(
            lambda: on(condition, lambda: remote(t, what, block, part, target).wait_send())
        )

    def take(t, what, block, part, condition=None):
        on(condition, lambda: remote(t, what, block, part, sibling).wait_recv())

    quarter = CHUNK // 4
    loop_parts = [
        (0,),
        (1, pl.ds(2 * quarter, 2 * quarter)),
        (1, pl.ds(quarter, quarter)),
        (1, pl.ds(0, quarter)),
    ]
    middle = jnp.where(outer, 1, -1)
    loop_way = [-away, -away, -away * middle, away]

    def first_hop(t):
        own = slot(x, z)
        send(t, ZP, own, (0,), node(x, z + 1))
        send(t, ZM + 1, own, (1,), node(x, z + 3))
        send(t, ZP + 1, own, (1,), node(x, z + 1), z != 3)
        send(t, ZM, own, (0,), node(x, z + 3), z != 0)
        for i, part in enumerate(loop_parts):
            send(t, LA + i, own, part, node(x + loop_way[i] + 4, z))
        send(t, SB, own, (), sibling)

    def second_hop(t):
        below, above = slot(x, z + 3), slot(x, z + 1)
        take(t, ZP, below, (0,))
        send(t, ZA, below, (0,), node(x, z + 1), z != 2)
        take(t, ZM + 1, above, (1,))
        send(t, ZB, above, (1,), node(x, z + 3), z != 1)
        take(t, ZP + 1, below, (1,), z != 0)
        take(t, ZM, above, (0,), z != 3)
        side = z // 3
        send(
            t,
            ZC,
            slot(x, z + 1 + 2 * side),
            (side,),
            node(x, z + 3 + 2 * side),
            outer,
        )
        send(t, XE, slot(x, 3 - z), (side,), node(x + away + 4, z), outer & gives)
        send(t, SB + 1, below, (), sibling, z != 0)
        send(t, SB + 2, above, (), sibling, z != 3)

    def loop_hop(t):
        for i, part in enumerate(loop_parts):
            block = slot(x - loop_way[i] + 4, z)
            take(t, LA + i, block, part)
            send(t, LB + i, block, part, node(x + loop_way[i] + 4, z))

    def cross(t):
        far = slot(x, z + 2)
        side = z // 3
        on(z != 3, lambda: remote(t, ZA, far, (0,), sibling).wait_recv())
        on(z != 0, lambda: remote(t, ZB, far, (1,), sibling).wait_recv())
        on(outer, lambda: remote(t, ZC, far, (1 - side,), sibling).wait_recv())
        for s in range(SEG):
            send(t, XN + s, far, (s,), node(x + away + 4, z), gives)
        send(t, SB + 3, far, (), sibling, core == z // 2)

    def crossed(t):
        near = slot(x - away + 4, z + 2)
        for s in range(SEG):
            take(t, XN + s, near, (s,), takes)
        inner = jnp.logical_not(outer)
        send(t, ZE, near, (jnp.clip(2 - z, 0, 1),), node(x, 3 * (z // 2)), inner & takes)
        send(t, SB + 4, near, (), sibling, takes & (core == 1 - z // 2))

    def last_hop(t):
        edge = slot(x - away + 4, 3 - z)
        side = z // 3
        take(t, XE, edge, (side,), outer & takes)
        take(t, ZE, edge, (1 - side,), outer & takes)
        send(t, SB + 5, edge, (), sibling, outer & takes)

    def settle(t):
        other = 1 - core
        for i in range(len(loop_parts)):
            take(t, LB + i, slot(x + 2, z), loop_parts[i])
        take(t, SB, slot(x, z, other), ())
        take(t, SB + 1, slot(x, z + 3, other), (), z != 0)
        take(t, SB + 2, slot(x, z + 1, other), (), z != 3)
        take(t, SB + 3, slot(x, z + 2, other), (), other == z // 2)
        take(t, SB + 4, slot(x - away + 4, z + 2, other), (), takes & (other == 1 - z // 2))
        take(t, SB + 5, slot(x - away + 4, 3 - z, other), (), outer & takes)

    def rotate(block, sign):
        real, imag = block[:, :NF].astype(F32), block[:, NF:].astype(F32)
        cos1, sin1 = small[0:1, :], small[1:2, :] * sign
        cos2, sin2 = small[2:3, :], small[3:4, :] * sign
        rc, ic, rs, js = real * cos1, imag * cos1, real * sin1, imag * sin1
        back2 = (real * cos2 + imag * sin2, imag * cos2 - real * sin2)
        back1 = (rc + js, ic - rs)
        ahead = (rc - js, ic + rs)
        return back2, back1, None, ahead

    def gather_rows(block, s, chunks):
        parts = [pools[t][block, s] for t in chunks]
        return parts[0] if len(parts) == 1 else jnp.concatenate(parts, axis=0)

    def correlate(g):
        group = GROUPS[g]
        new, old, shapes = regions(group)
        earlier = tuple(range(group[0]))

        def product(first, second, chunks, sign):
            total = None
            for s in range(SEG):
                for i, t in enumerate(group):
                    block = pools[t][first, s]
                    for m, turned in enumerate(rotate(block, sign)):
                        at = m * new + i * CHUNK
                        if turned is None:
                            rot[s, at : at + CHUNK] = block
                        else:
                            rot[s, at : at + CHUNK, :NF] = turned[0].astype(BF16)
                            rot[s, at : at + CHUNK, NF:] = turned[1].astype(BF16)
                term = lax.dot_general(
                    rot[s, : NLAG * new],
                    gather_rows(second, s, chunks),
                    (((1,), (1,)), ((), ())),
                    preferred_element_type=F32,
                )
                total = term if total is None else total + term
            return total

        def one_pair(p, carry):
            first, second = pairs[p, 0], pairs[p, 1]
            todo = [(first, second, earlier + group, 1.0)]
            if old:
                todo.append((second, first, earlier, -1.0))
            for r, (a, b, chunks, sign) in enumerate(todo):
                total = product(a, b, chunks, sign)
                wide = total.shape[1]
                for m in range(NLAG):
                    sends[g][r][m, p, :, :wide] = total[m * new : (m + 1) * new].astype(BF16)
                    if wide < shapes[r][1]:
                        sends[g][r][m, p, :, wide:] = jnp.zeros((new, shapes[r][1] - wide), BF16)
                for d in (2, 1, 3):
                    across(g, r, d, p).start()
            return carry

        lax.fori_loop(0, PAIRS, one_pair, 0)

    def across(g, r, d, p):
        place = sum(spans[:g]) + r
        lag = (y + d) % 4
        return pltpu.make_async_remote_copy(
            src_ref=sends[g][r].at[lag, p],
            dst_ref=lands[g][r].at[d - 1, p],
            send_sem=ysem.at[place, d - 1, p],
            recv_sem=yrsem.at[place, d - 1, p],
            device_id=(h, lag),
            device_id_type=MESH,
        )

    def finish(g):
        new, old, shapes = regions(GROUPS[g])
        scale = 1.0 / math.sqrt(NF * SEG * 4)

        def one_pair(p, carry):
            for r in range(len(shapes)):
                total = sends[g][r][y, p].astype(F32)
                for d in (1, 2, 3):
                    across(g, r, d, p).wait_recv()
                    total += lands[g][r][d - 1, p].astype(F32)
                total *= scale
                if r == 0:
                    out[0, p, old : old + new, : old + new] = total[:, : old + new]
                else:
                    out[0, p, :old, old : old + new] = total.T[:old]
            return carry

        lax.fori_loop(0, PAIRS, one_pair, 0)

    spectra(0)
    pl.semaphore_wait(barrier, len(partners))
    first_hop(0)
    spectra(1)
    first_hop(1)
    spectra(2)
    spectra(3)
    second_hop(0)
    loop_hop(0)
    first_hop(2)
    cross(0)
    second_hop(1)
    loop_hop(1)
    first_hop(3)
    cross(1)
    crossed(0)
    second_hop(2)
    loop_hop(2)
    last_hop(0)
    settle(0)
    cross(2)
    crossed(1)
    second_hop(3)
    loop_hop(3)
    last_hop(1)
    settle(1)
    cross(3)
    correlate(0)
    crossed(2)
    last_hop(2)
    settle(2)
    crossed(3)
    correlate(1)
    last_hop(3)
    settle(3)
    correlate(2)
    for g in range(len(GROUPS)):
        finish(g)
    for done in started:
        done()

    def sent(p, carry):
        for g in range(len(GROUPS)):
            for r in range(spans[g]):
                for d in (1, 2, 3):
                    across(g, r, d, p).wait_send()
        return carry

    lax.fori_loop(0, PAIRS, sent, 0)


def local(traces, pairs):
    table, window, small = host_tables()
    scratch = [pltpu.VMEM((BLOCKS, SEG, CHUNK, 2 * NF), BF16) for _ in range(CHUNKS)]
    spans = 0
    for group in GROUPS:
        shapes = regions(group)[2]
        spans += len(shapes)
        scratch += [pltpu.VMEM((NLAG, PAIRS, *shape), BF16) for shape in shapes]
        scratch += [pltpu.VMEM((3, PAIRS, *shape), BF16) for shape in shapes]
    widest = max(len(group) for group in GROUPS) * CHUNK
    scratch += [
        pltpu.VMEM((CB, SEG, L), BF16),
        pltpu.VMEM((L, 2 * NF), BF16),
        pltpu.VMEM((2 * NF // 128, SEG * CHUNK, 128), F32),
        pltpu.VMEM((SEG, NLAG * widest, 2 * NF), BF16),
        pltpu.SemaphoreType.DMA((CHUNKS + TABLE_CUTS,)),
        pltpu.SemaphoreType.DMA((CHUNKS, COPIES)),
        pltpu.SemaphoreType.DMA((CHUNKS, COPIES)),
        pltpu.SemaphoreType.DMA((spans, 3, PAIRS)),
        pltpu.SemaphoreType.DMA((spans, 3, PAIRS)),
    ]
    return pl.pallas_call(
        kernel,
        out_shape=jax.ShapeDtypeStruct((1, PAIRS, CB, CB), F32),
        in_specs=[
            pl.BlockSpec(memory_space=pl.ANY),
            pl.BlockSpec(memory_space=pl.ANY),
            pl.BlockSpec(memory_space=pltpu.VMEM),
            pl.BlockSpec(memory_space=pltpu.VMEM),
            pl.BlockSpec(memory_space=pltpu.SMEM),
        ],
        out_specs=pl.BlockSpec(memory_space=pltpu.VMEM),
        scratch_shapes=scratch,
        compiler_params=pltpu.CompilerParams(
            collective_id=0, has_side_effects=True, vmem_limit_bytes=62 << 20
        ),
        name="correlate_pairs",
    )(traces, jnp.asarray(table), jnp.asarray(window), jnp.asarray(small), pairs)


def solution(mesh):
    placed = (P("chan", "seg", None), P("chan", None))
    return jax.shard_map(
        local, mesh=mesh, in_specs=placed, out_specs=P("seg", "chan", None, None), check_vma=False
    )
```

```python
import math

import jax
import jax.numpy as jnp
import numpy as np
from jax import lax
from jax.experimental import pallas as pl
from jax.experimental.pallas import tpu as pltpu
from jax.sharding import PartitionSpec as P

CB = 256
L = 4096
NF = 512
FLO = 64
HW = 64
LAGSTEP = 16
NLAG = 4
PAIRS = 4
BLOCKS = 32
SEG = 2
SIZES = (64, 64, 64, 64)
CHUNKS = len(SIZES)
STARTS = tuple(sum(SIZES[:t]) for t in range(CHUNKS))
GROUPS = ((0, 1), (2,), (3,))
TABLE_CUTS = 8
AHEAD = 7
MESH = pl.DeviceIdType.MESH
BF16 = jnp.bfloat16
F32 = jnp.float32

ORDER = (
    "S0", "Z0", "O0", "S1", "S2", "S3", "Z1", "O2", "O1", "O3", "B1", "M0", "B0", "H0", "I0",
    "M2", "H1", "I1", "X0", "L0", "Z2", "X1", "C0", "B3", "H2", "B2", "I2", "L1", "Z3", "E0",
    "T0", "M1", "X2", "C1", "H3", "L2", "I3", "E1", "T1", "K00", "K01", "K02", "K03", "X3", "C2",
    "L3", "E2", "T2", "K10", "K11", "K12", "K13", "M3", "C3", "E3", "T3", "K20", "K21", "K22",
    "K23", "G0", "G1", "G2",
)

LAST = "K" + str(len(GROUPS) - 1) + str(PAIRS - 1)

ZP, ZM, ZA, ZB, ZC, XN, XE, ZE, LA, LB, SB = 0, 2, 4, 5, 6, 7, 9, 10, 11, 15, 19
COPIES = 25


def host_tables():
    sample = np.arange(L)
    bins = FLO + np.arange(NF)
    angles = 2.0 * np.pi / L * ((sample[:, None] * bins[None, :]) % L)
    taper = (0.5 - 0.5 * np.cos(2.0 * np.pi / L * sample))[:, None] / math.sqrt(L)
    table = np.concatenate([taper * np.cos(angles), -taper * np.sin(angles)], axis=1)
    rows = np.arange(NF)
    window = np.abs(rows[:, None] - rows[None, :]) <= HW
    phase = 2.0 * np.pi / L * ((LAGSTEP * bins) % L)
    small = np.zeros((8, NF), np.float32)
    small[0], small[1] = np.cos(phase), np.sin(phase)
    small[2], small[3] = np.cos(2.0 * phase), np.sin(2.0 * phase)
    small[4] = 1.0 / window.sum(axis=0)
    return table.astype(BF16), window.astype(BF16), small


def regions(group):
    new = sum(SIZES[t] for t in group)
    old = STARTS[group[0]]
    shapes = [(new, -(-(old + new) // 128) * 128)]
    if old:
        shapes.append((new, -(-old // 128) * 128))
    return new, old, shapes


def kernel(traces, table_hbm, window_hbm, small_hbm, pairs, result, *scratch):
    pools = scratch[:CHUNKS]
    scratch = scratch[CHUNKS:]
    spans = [len(regions(group)[2]) for group in GROUPS]
    sends, lands = [], []
    for span in spans:
        sends.append(scratch[:span])
        lands.append(scratch[span : 2 * span])
        scratch = scratch[2 * span :]
    rows_in, table, window, small, white, rot, out, in_sem, ssem, rsem, ysem, yrsem = scratch

    h = lax.axis_index("chan")
    y = lax.axis_index("seg")
    core = h % 2
    z = (h // 2) % 4
    x = h // 8
    away = 1 - 2 * (z // 2)
    outer = (z == 0) | (z == 3)
    gives = (x + away >= 0) & (x + away <= 3)
    takes = (x - away >= 0) & (x - away <= 3)

    def node(xx, zz, cc=None):
        return ((xx % 4) * 8 + (zz % 4) * 2 + (core if cc is None else cc), y)

    def slot(xx, zz, cc=None):
        return node(xx, zz, cc)[0]

    sibling = node(x, z, 1 - core)
    partners = [node(x, z + 1), node(x, z + 3), node(x + 1, z), node(x + 3, z), sibling]
    partners += [(h, (y + d) % 4) for d in (1, 2, 3)]

    fetch_rows = [
        pltpu.make_async_copy(
            traces.at[pl.ds(STARTS[t], SIZES[t])],
            rows_in.at[pl.ds(STARTS[t], SIZES[t])],
            in_sem.at[t],
        )
        for t in range(CHUNKS)
    ]
    cut = L // TABLE_CUTS
    fetch_table = [
        pltpu.make_async_copy(
            table_hbm.at[pl.ds(i * cut, cut)], table.at[pl.ds(i * cut, cut)], in_sem.at[CHUNKS + i]
        )
        for i in range(TABLE_CUTS)
    ]
    fetch_small = [
        pltpu.make_async_copy(window_hbm, window, in_sem.at[CHUNKS + TABLE_CUTS]),
        pltpu.make_async_copy(small_hbm, small, in_sem.at[CHUNKS + TABLE_CUTS + 1]),
    ]
    fetches = [fetch_rows[0], *fetch_table, *fetch_small, *fetch_rows[1:]]
    for copy in fetches[:AHEAD]:
        copy.start()

    barrier = pltpu.get_barrier_semaphore()
    for partner in partners:
        pl.semaphore_signal(barrier, inc=1, device_id=partner, device_id_type=MESH)

    def spectra(t):
        fetch_rows[t].wait()
        size = SIZES[t]
        rows = rows_in[STARTS[t] : STARTS[t] + size].reshape(SEG * size, L)
        if t == 0:
            spec = jnp.zeros((SEG * size, 2 * NF), F32)
            for i in range(TABLE_CUTS):
                fetch_table[i].wait()
                for copy in fetches[i + AHEAD : i + AHEAD + 1]:
                    copy.start()
                spec += jnp.dot(
                    rows[:, i * cut : (i + 1) * cut],
                    table[i * cut : (i + 1) * cut],
                    preferred_element_type=F32,
                )
        else:
            spec = jnp.dot(rows, table[...], preferred_element_type=F32)
        if t == 0:
            for copy in fetch_small:
                copy.wait()
        real, imag = spec[:, :NF], spec[:, NF:]
        power = real * real + imag * imag
        high = power.astype(BF16)
        low = (power - high.astype(F32)).astype(BF16)
        smooth = jnp.dot(high, window[...], preferred_element_type=F32)
        smooth += jnp.dot(low, window[...], preferred_element_type=F32)
        factor = lax.rsqrt(smooth * small[4:5, :] + 1e-06)
        for j in range(2 * NF // 128):
            part = real if j * 128 < NF else imag
            lanes = slice(j * 128 % NF, j * 128 % NF + 128)
            white[j, : SEG * size] = part[:, lanes] * factor[:, lanes]
            for s in range(SEG):
                rows = white[j, pl.ds(s, size, stride=SEG), :]
                pools[t][h, s, :, j * 128 : (j + 1) * 128] = rows.astype(BF16)

    started = []

    def remote(t, what, block, part, target):
        view = pools[t].at[(block, *part)]
        return pltpu.make_async_remote_copy(
            src_ref=view,
            dst_ref=view,
            send_sem=ssem.at[t, what],
            recv_sem=rsem.at[t, what],
            device_id=target,
            device_id_type=MESH,
        )

    def on(condition, act):
        if condition is None:
            act()
        else:
            pl.when(condition)(act)

    def send(t, what, block, part, target, condition=None):
        on(condition, lambda: remote(t, what, block, part, target).start())
        started.append(
            lambda: on(condition, lambda: remote(t, what, block, part, target).wait_send())
        )

    def take(t, what, block, part, condition=None):
        on(condition, lambda: remote(t, what, block, part, sibling).wait_recv())

    def loop_parts(t):
        size = SIZES[t]
        low = max(size // 4, 16)
        cuts = [(0,), (1, pl.ds(size // 2, size // 2))]
        if low < size // 2:
            cuts.append((1, pl.ds(low, size // 2 - low)))
        cuts.append((1, pl.ds(0, low)))
        return list(zip(cuts, loop_way))

    middle = jnp.where(outer, 1, -1)
    loop_way = [-away, -away, -away * middle, away]

    def ring(t):
        own = slot(x, z)
        send(t, ZP, own, (0,), node(x, z + 1))
        send(t, ZM + 1, own, (1,), node(x, z + 3))
        send(t, ZP + 1, own, (1,), node(x, z + 1), z != 3)
        send(t, ZM, own, (0,), node(x, z + 3), z != 0)

    def loop(t):
        for i, (part, way) in enumerate(loop_parts(t)):
            send(t, LA + i, slot(x, z), part, node(x + way + 4, z))

    def share(t):
        send(t, SB, slot(x, z), (), sibling)

    def ring_on(t):
        below, above = slot(x, z + 3), slot(x, z + 1)
        take(t, ZP, below, (0,))
        send(t, ZA, below, (0,), node(x, z + 1), z != 2)
        take(t, ZM + 1, above, (1,))
        send(t, ZB, above, (1,), node(x, z + 3), z != 1)

    def ring_rest(t):
        below, above = slot(x, z + 3), slot(x, z + 1)
        take(t, ZP + 1, below, (1,), z != 0)
        take(t, ZM, above, (0,), z != 3)
        side = z // 3
        send(t, ZC, slot(x, z + 1 + 2 * side), (side,), node(x, z + 3 + 2 * side), outer)
        send(t, XE, slot(x, 3 - z), (side,), node(x + away + 4, z), outer & gives)
        send(t, SB + 1, below, (), sibling, z != 0)
        send(t, SB + 2, above, (), sibling, z != 3)

    def loop_on(t, which):
        for i, (part, way) in enumerate(loop_parts(t)):
            if i in which:
                block = slot(x - way + 4, z)
                take(t, LA + i, block, part)
                send(t, LB + i, block, part, node(x + way + 4, z))

    def cross(t):
        far = slot(x, z + 2)
        side = z // 3
        on(z != 3, lambda: remote(t, ZA, far, (0,), sibling).wait_recv())
        on(z != 0, lambda: remote(t, ZB, far, (1,), sibling).wait_recv())
        on(outer, lambda: remote(t, ZC, far, (1 - side,), sibling).wait_recv())
        for s in range(SEG):
            send(t, XN + s, far, (s,), node(x + away + 4, z), gives)
        send(t, SB + 3, far, (), sibling, core == z // 2)

    def crossed(t):
        near = slot(x - away + 4, z + 2)
        for s in range(SEG):
            take(t, XN + s, near, (s,), takes)
        inner = jnp.logical_not(outer)
        send(t, ZE, near, (jnp.clip(2 - z, 0, 1),), node(x, 3 * (z // 2)), inner & takes)
        send(t, SB + 4, near, (), sibling, takes & (core == 1 - z // 2))

    def last_hop(t):
        edge = slot(x - away + 4, 3 - z)
        side = z // 3
        take(t, XE, edge, (side,), outer & takes)
        take(t, ZE, edge, (1 - side,), outer & takes)
        send(t, SB + 5, edge, (), sibling, outer & takes)

    def settle(t):
        other = 1 - core
        for i, (part, _) in enumerate(loop_parts(t)):
            take(t, LB + i, slot(x + 2, z), part)
        take(t, SB, slot(x, z, other), ())
        take(t, SB + 1, slot(x, z + 3, other), (), z != 0)
        take(t, SB + 2, slot(x, z + 1, other), (), z != 3)
        take(t, SB + 3, slot(x, z + 2, other), (), other == z // 2)
        take(t, SB + 4, slot(x - away + 4, z + 2, other), (), takes & (other == 1 - z // 2))
        take(t, SB + 5, slot(x - away + 4, 3 - z, other), (), outer & takes)

    def rotate(block, sign):
        real, imag = block[:, :NF].astype(F32), block[:, NF:].astype(F32)
        cos1, sin1 = small[0:1, :], small[1:2, :] * sign
        cos2, sin2 = small[2:3, :], small[3:4, :] * sign
        rc, ic, rs, js = real * cos1, imag * cos1, real * sin1, imag * sin1
        back2 = (real * cos2 + imag * sin2, imag * cos2 - real * sin2)
        back1 = (rc + js, ic - rs)
        ahead = (rc - js, ic + rs)
        return back2, back1, None, ahead

    def gather_rows(block, s, chunks):
        parts = [pools[t][block, s] for t in chunks]
        return parts[0] if len(parts) == 1 else jnp.concatenate(parts, axis=0)

    def correlate(g, low, high):
        group = GROUPS[g]
        new, old, shapes = regions(group)
        earlier = tuple(range(group[0]))

        def product(first, second, chunks, sign):
            total = None
            for s in range(SEG):
                for t in group:
                    block = pools[t][first, s]
                    for m, turned in enumerate(rotate(block, sign)):
                        at = m * new + STARTS[t] - old
                        end = at + SIZES[t]
                        if turned is None:
                            rot[s, at:end] = block
                        else:
                            rot[s, at:end, :NF] = turned[0].astype(BF16)
                            rot[s, at:end, NF:] = turned[1].astype(BF16)
                term = lax.dot_general(
                    rot[s, : NLAG * new],
                    gather_rows(second, s, chunks),
                    (((1,), (1,)), ((), ())),
                    preferred_element_type=F32,
                )
                total = term if total is None else total + term
            return total

        def one_pair(p, carry):
            first, second = pairs[0, p], pairs[1, p]
            todo = [(first, second, earlier + group, 1.0)]
            if old:
                todo.append((second, first, earlier, -1.0))
            for r, (a, b, chunks, sign) in enumerate(todo):
                total = product(a, b, chunks, sign)
                wide = total.shape[1]
                for m in range(NLAG):
                    sends[g][r][m, p, :, :wide] = total[m * new : (m + 1) * new].astype(BF16)
                    if wide < shapes[r][1]:
                        sends[g][r][m, p, :, wide:] = jnp.zeros((new, shapes[r][1] - wide), BF16)
                for d in (2, 1, 3):
                    across(g, r, d, p).start()
            return carry

        run(one_pair, low, high)

    def run(body, low, high):
        if high - low == 1:
            body(low, 0)
        else:
            lax.fori_loop(low, high, body, 0)

    def across(g, r, d, p):
        place = sum(spans[:g]) + r
        lag = (y + d) % 4
        return pltpu.make_async_remote_copy(
            src_ref=sends[g][r].at[lag, p],
            dst_ref=lands[g][r].at[d - 1, p],
            send_sem=ysem.at[place, d - 1, p],
            recv_sem=yrsem.at[place, d - 1, p],
            device_id=(h, lag),
            device_id_type=MESH,
        )

    def store(p):
        sem = in_sem.at[CHUNKS + TABLE_CUTS + 2 + p]
        return pltpu.make_async_copy(out.at[p], result.at[0, p], sem)

    def finish(g):
        new, old, shapes = regions(GROUPS[g])
        scale = 1.0 / math.sqrt(NF * SEG * 4)

        def one_pair(p, carry):
            for r in range(spans[g]):
                total = sends[g][r][y, p].astype(F32)
                for d in (1, 3, 2):
                    across(g, r, d, p).wait_recv()
                    total += lands[g][r][d - 1, p].astype(F32)
                total *= scale
                if r == 0:
                    out[p, old : old + new, : old + new] = total[:, : old + new]
                else:
                    out[p, :old, old : old + new] = total.T[:old]
                for d in (1, 2, 3):
                    across(g, r, d, p).wait_send()
            if g == len(GROUPS) - 1:
                store(p).start()
            return carry

        lax.fori_loop(0, PAIRS, one_pair, 0)

    steps = {
        "S": spectra,
        "Z": ring,
        "O": loop,
        "B": share,
        "H": ring_on,
        "I": ring_rest,
        "L": lambda t: loop_on(t, (0, 1)),
        "M": lambda t: loop_on(t, (2, 3)),
        "X": cross,
        "C": crossed,
        "E": last_hop,
        "T": settle,
        "G": finish,
    }
    at = 0
    while at < len(ORDER):
        step = ORDER[at]
        at += 1
        if step[0] == "K":
            g, low = int(step[1]), int(step[2])
            high = low + 1
            while at < len(ORDER) and ORDER[at] == step[:2] + str(high):
                high += 1
                at += 1
            correlate(g, low, high)
            step = "K" + str(g) + str(high - 1)
        else:
            steps[step[0]](int(step[1]))
        if step == LAST:
            for done in started:
                done()
        if step == "S0":
            pl.semaphore_wait(barrier, len(partners))

    for p in range(PAIRS):
        store(p).wait()


def local(traces, pairs):
    table, window, small = host_tables()
    scratch = [pltpu.VMEM((BLOCKS, SEG, size, 2 * NF), BF16) for size in SIZES]
    spans = 0
    for group in GROUPS:
        shapes = regions(group)[2]
        spans += len(shapes)
        scratch += [pltpu.VMEM((NLAG, PAIRS, *shape), BF16) for shape in shapes]
        scratch += [pltpu.VMEM((3, PAIRS, *shape), BF16) for shape in shapes]
    widest = max(regions(group)[0] for group in GROUPS)
    scratch += [
        pltpu.VMEM((CB, SEG, L), BF16),
        pltpu.VMEM((L, 2 * NF), BF16),
        pltpu.VMEM((NF, NF), BF16),
        pltpu.VMEM((8, NF), F32),
        pltpu.VMEM((2 * NF // 128, SEG * max(SIZES), 128), F32),
        pltpu.VMEM((SEG, NLAG * widest, 2 * NF), BF16),
        pltpu.VMEM((PAIRS, CB, CB), F32),
        pltpu.SemaphoreType.DMA((CHUNKS + TABLE_CUTS + 2 + PAIRS,)),
        pltpu.SemaphoreType.DMA((CHUNKS, COPIES)),
        pltpu.SemaphoreType.DMA((CHUNKS, COPIES)),
        pltpu.SemaphoreType.DMA((spans, 3, PAIRS)),
        pltpu.SemaphoreType.DMA((spans, 3, PAIRS)),
    ]
    return pl.pallas_call(
        kernel,
        out_shape=jax.ShapeDtypeStruct((1, PAIRS, CB, CB), F32),
        in_specs=[
            pl.BlockSpec(memory_space=pl.ANY),
            pl.BlockSpec(memory_space=pl.ANY),
            pl.BlockSpec(memory_space=pl.ANY),
            pl.BlockSpec(memory_space=pl.ANY),
            pl.BlockSpec(memory_space=pltpu.SMEM),
        ],
        out_specs=pl.BlockSpec(memory_space=pl.ANY),
        scratch_shapes=scratch,
        compiler_params=pltpu.CompilerParams(
            collective_id=0, has_side_effects=True, vmem_limit_bytes=62 << 20
        ),
        name="correlate_pairs",
    )(traces, jnp.asarray(table), jnp.asarray(window), jnp.asarray(small), pairs.T)


def solution(mesh):
    placed = (P("chan", "seg", None), P("chan", None))
    return jax.shard_map(
        local, mesh=mesh, in_specs=placed, out_specs=P("seg", "chan", None, None), check_vma=False
    )
```

```python
import math

import jax
import jax.numpy as jnp
import numpy as np
from jax import lax
from jax.experimental import pallas as pl
from jax.experimental.pallas import tpu as pltpu
from jax.sharding import PartitionSpec as P

CB = 256
L = 4096
NF = 512
FLO = 64
HW = 64
LAGSTEP = 16
NLAG = 4
PAIRS = 4
BLOCKS = 32
SEG = 2
SIZES = (64, 64, 64, 64)
CHUNKS = len(SIZES)
STARTS = tuple(sum(SIZES[:t]) for t in range(CHUNKS))
GROUPS = ((0, 1), (2,), (3,))
TABLE_CUTS = 8
AHEAD = 7
MESH = pl.DeviceIdType.MESH
BF16 = jnp.bfloat16
F32 = jnp.float32

ORDER = (
    "S0", "Z0", "O0", "S1", "B1", "S2", "S3", "O2", "M0", "Z1", "O3", "B2", "O1", "H0", "I0",
    "M2", "L0", "H1", "I1", "X0", "Z2", "X1", "M1", "C0", "H2", "I2", "L1", "B3", "Z3", "X2",
    "B0", "E0", "T0", "C1", "L2", "H3", "I3", "E1", "T1", "K00", "K01", "K02", "C2", "E2", "K03",
    "X3", "L3", "T2", "K10", "K11", "G0", "K12", "K13", "M3", "C3", "E3", "T3", "K20", "K21",
    "K22", "K23", "G1", "G2",
)

LAST = "K" + str(len(GROUPS) - 1) + str(PAIRS - 1)

ZP, ZM, ZA, ZB, ZC, XN, XE, ZE, LA, LB, SB = 0, 2, 4, 5, 6, 7, 9, 10, 11, 15, 19
COPIES = 25


def host_tables():
    sample = np.arange(L)
    bins = FLO + np.arange(NF)
    angles = 2.0 * np.pi / L * ((sample[:, None] * bins[None, :]) % L)
    taper = (0.5 - 0.5 * np.cos(2.0 * np.pi / L * sample))[:, None] / math.sqrt(L)
    table = np.concatenate([taper * np.cos(angles), -taper * np.sin(angles)], axis=1)
    rows = np.arange(NF)
    window = np.abs(rows[:, None] - rows[None, :]) <= HW
    phase = 2.0 * np.pi / L * ((LAGSTEP * bins) % L)
    small = np.zeros((8, NF), np.float32)
    small[0], small[1] = np.cos(phase), np.sin(phase)
    small[2], small[3] = np.cos(2.0 * phase), np.sin(2.0 * phase)
    small[4] = 1.0 / window.sum(axis=0)
    return table.astype(BF16), window.astype(BF16), small


def regions(group):
    new = sum(SIZES[t] for t in group)
    old = STARTS[group[0]]
    shapes = [(new, -(-(old + new) // 128) * 128)]
    if old:
        shapes.append((new, -(-old // 128) * 128))
    return new, old, shapes


def kernel(traces, table_hbm, window_hbm, small_hbm, pairs, result, *scratch):
    pools = scratch[:CHUNKS]
    scratch = scratch[CHUNKS:]
    spans = [len(regions(group)[2]) for group in GROUPS]
    sends, lands = [], []
    for span in spans:
        sends.append(scratch[:span])
        lands.append(scratch[span : 2 * span])
        scratch = scratch[2 * span :]
    rows_in, table, window, small, white, rot, out, in_sem, ssem, rsem, ysem, yrsem = scratch

    h = lax.axis_index("chan")
    y = lax.axis_index("seg")
    core = h % 2
    z = (h // 2) % 4
    x = h // 8
    away = 1 - 2 * (z // 2)
    outer = (z == 0) | (z == 3)
    gives = (x + away >= 0) & (x + away <= 3)
    takes = (x - away >= 0) & (x - away <= 3)

    def node(xx, zz, cc=None):
        return ((xx % 4) * 8 + (zz % 4) * 2 + (core if cc is None else cc), y)

    def slot(xx, zz, cc=None):
        return node(xx, zz, cc)[0]

    sibling = node(x, z, 1 - core)
    partners = [node(x, z + 1), node(x, z + 3), node(x + 1, z), node(x + 3, z), sibling]
    partners += [(h, (y + d) % 4) for d in (1, 2, 3)]

    fetch_rows = [
        pltpu.make_async_copy(
            traces.at[pl.ds(STARTS[t], SIZES[t])],
            rows_in.at[pl.ds(STARTS[t], SIZES[t])],
            in_sem.at[t],
        )
        for t in range(CHUNKS)
    ]
    cut = L // TABLE_CUTS
    fetch_table = [
        pltpu.make_async_copy(
            table_hbm.at[pl.ds(i * cut, cut)], table.at[pl.ds(i * cut, cut)], in_sem.at[CHUNKS + i]
        )
        for i in range(TABLE_CUTS)
    ]
    fetch_small = [
        pltpu.make_async_copy(window_hbm, window, in_sem.at[CHUNKS + TABLE_CUTS]),
        pltpu.make_async_copy(small_hbm, small, in_sem.at[CHUNKS + TABLE_CUTS + 1]),
    ]
    fetches = [fetch_rows[0], *fetch_table, *fetch_small, *fetch_rows[1:]]
    for copy in fetches[:AHEAD]:
        copy.start()

    barrier = pltpu.get_barrier_semaphore()
    for partner in partners:
        pl.semaphore_signal(barrier, inc=1, device_id=partner, device_id_type=MESH)

    def spectra(t):
        fetch_rows[t].wait()
        size = SIZES[t]
        rows = rows_in[STARTS[t] : STARTS[t] + size].reshape(SEG * size, L)
        if t == 0:
            spec = jnp.zeros((SEG * size, 2 * NF), F32)
            for i in range(TABLE_CUTS):
                fetch_table[i].wait()
                for copy in fetches[i + AHEAD : i + AHEAD + 1]:
                    copy.start()
                spec += jnp.dot(
                    rows[:, i * cut : (i + 1) * cut],
                    table[i * cut : (i + 1) * cut],
                    preferred_element_type=F32,
                )
        else:
            spec = jnp.dot(rows, table[...], preferred_element_type=F32)
        if t == 0:
            for copy in fetch_small:
                copy.wait()
        real, imag = spec[:, :NF], spec[:, NF:]
        power = real * real + imag * imag
        high = power.astype(BF16)
        low = (power - high.astype(F32)).astype(BF16)
        smooth = jnp.dot(high, window[...], preferred_element_type=F32)
        smooth += jnp.dot(low, window[...], preferred_element_type=F32)
        factor = lax.rsqrt(smooth * small[4:5, :] + 1e-06)
        for j in range(2 * NF // 128):
            part = real if j * 128 < NF else imag
            lanes = slice(j * 128 % NF, j * 128 % NF + 128)
            white[j, : SEG * size] = part[:, lanes] * factor[:, lanes]
            for s in range(SEG):
                rows = white[j, pl.ds(s, size, stride=SEG), :]
                pools[t][h, s, :, j * 128 : (j + 1) * 128] = rows.astype(BF16)

    started = []

    def remote(t, what, block, part, target):
        view = pools[t].at[(block, *part)]
        return pltpu.make_async_remote_copy(
            src_ref=view,
            dst_ref=view,
            send_sem=ssem.at[t, what],
            recv_sem=rsem.at[t, what],
            device_id=target,
            device_id_type=MESH,
        )

    def on(condition, act):
        if condition is None:
            act()
        else:
            pl.when(condition)(act)

    def send(t, what, block, part, target, condition=None):
        on(condition, lambda: remote(t, what, block, part, target).start())
        started.append(
            lambda: on(condition, lambda: remote(t, what, block, part, target).wait_send())
        )

    def take(t, what, block, part, condition=None):
        on(condition, lambda: remote(t, what, block, part, sibling).wait_recv())

    def loop_parts(t):
        size = SIZES[t]
        low = max(size // 4, 16)
        cuts = [(0,), (1, pl.ds(size // 2, size // 2))]
        if low < size // 2:
            cuts.append((1, pl.ds(low, size // 2 - low)))
        cuts.append((1, pl.ds(0, low)))
        return list(zip(cuts, loop_way))

    middle = jnp.where(outer, 1, -1)
    loop_way = [-away, -away, -away * middle, away]

    def ring(t):
        own = slot(x, z)
        send(t, ZP, own, (0,), node(x, z + 1))
        send(t, ZM + 1, own, (1,), node(x, z + 3))
        send(t, ZP + 1, own, (1,), node(x, z + 1), z != 3)
        send(t, ZM, own, (0,), node(x, z + 3), z != 0)

    def loop(t):
        for i, (part, way) in enumerate(loop_parts(t)):
            send(t, LA + i, slot(x, z), part, node(x + way + 4, z))

    def share(t):
        send(t, SB, slot(x, z), (), sibling)

    def ring_on(t):
        below, above = slot(x, z + 3), slot(x, z + 1)
        take(t, ZP, below, (0,))
        send(t, ZA, below, (0,), node(x, z + 1), z != 2)
        take(t, ZM + 1, above, (1,))
        send(t, ZB, above, (1,), node(x, z + 3), z != 1)

    def ring_rest(t):
        below, above = slot(x, z + 3), slot(x, z + 1)
        take(t, ZP + 1, below, (1,), z != 0)
        take(t, ZM, above, (0,), z != 3)
        side = z // 3
        send(t, ZC, slot(x, z + 1 + 2 * side), (side,), node(x, z + 3 + 2 * side), outer)
        send(t, XE, slot(x, 3 - z), (side,), node(x + away + 4, z), outer & gives)
        send(t, SB + 1, below, (), sibling, z != 0)
        send(t, SB + 2, above, (), sibling, z != 3)

    def loop_on(t, which):
        for i, (part, way) in enumerate(loop_parts(t)):
            if i in which:
                block = slot(x - way + 4, z)
                take(t, LA + i, block, part)
                send(t, LB + i, block, part, node(x + way + 4, z))

    def cross(t):
        far = slot(x, z + 2)
        side = z // 3
        on(z != 3, lambda: remote(t, ZA, far, (0,), sibling).wait_recv())
        on(z != 0, lambda: remote(t, ZB, far, (1,), sibling).wait_recv())
        on(outer, lambda: remote(t, ZC, far, (1 - side,), sibling).wait_recv())
        for s in range(SEG):
            send(t, XN + s, far, (s,), node(x + away + 4, z), gives)
        send(t, SB + 3, far, (), sibling, core == z // 2)

    def crossed(t):
        near = slot(x - away + 4, z + 2)
        for s in range(SEG):
            take(t, XN + s, near, (s,), takes)
        inner = jnp.logical_not(outer)
        send(t, ZE, near, (jnp.clip(2 - z, 0, 1),), node(x, 3 * (z // 2)), inner & takes)
        send(t, SB + 4, near, (), sibling, takes & (core == 1 - z // 2))

    def last_hop(t):
        edge = slot(x - away + 4, 3 - z)
        side = z // 3
        take(t, XE, edge, (side,), outer & takes)
        take(t, ZE, edge, (1 - side,), outer & takes)
        send(t, SB + 5, edge, (), sibling, outer & takes)

    def settle(t):
        other = 1 - core
        for i, (part, _) in enumerate(loop_parts(t)):
            take(t, LB + i, slot(x + 2, z), part)
        take(t, SB, slot(x, z, other), ())
        take(t, SB + 1, slot(x, z + 3, other), (), z != 0)
        take(t, SB + 2, slot(x, z + 1, other), (), z != 3)
        take(t, SB + 3, slot(x, z + 2, other), (), other == z // 2)
        take(t, SB + 4, slot(x - away + 4, z + 2, other), (), takes & (other == 1 - z // 2))
        take(t, SB + 5, slot(x - away + 4, 3 - z, other), (), outer & takes)

    def rotate(block, sign):
        real, imag = block[:, :NF].astype(F32), block[:, NF:].astype(F32)
        cos1, sin1 = small[0:1, :], small[1:2, :] * sign
        cos2, sin2 = small[2:3, :], small[3:4, :] * sign
        rc, ic, rs, js = real * cos1, imag * cos1, real * sin1, imag * sin1
        back2 = (real * cos2 + imag * sin2, imag * cos2 - real * sin2)
        back1 = (rc + js, ic - rs)
        ahead = (rc - js, ic + rs)
        return back2, back1, None, ahead

    def gather_rows(block, s, chunks):
        parts = [pools[t][block, s] for t in chunks]
        return parts[0] if len(parts) == 1 else jnp.concatenate(parts, axis=0)

    def correlate(g, low, high):
        group = GROUPS[g]
        new, old, shapes = regions(group)
        earlier = tuple(range(group[0]))

        def product(first, second, chunks, sign):
            total = None
            for s in range(SEG):
                for t in group:
                    block = pools[t][first, s]
                    for m, turned in enumerate(rotate(block, sign)):
                        at = m * new + STARTS[t] - old
                        end = at + SIZES[t]
                        if turned is None:
                            rot[s, at:end] = block
                        else:
                            rot[s, at:end, :NF] = turned[0].astype(BF16)
                            rot[s, at:end, NF:] = turned[1].astype(BF16)
                term = lax.dot_general(
                    rot[s, : NLAG * new],
                    gather_rows(second, s, chunks),
                    (((1,), (1,)), ((), ())),
                    preferred_element_type=F32,
                )
                total = term if total is None else total + term
            return total

        def one_pair(p, carry):
            first, second = pairs[0, p], pairs[1, p]
            todo = [(first, second, earlier + group, 1.0)]
            if old:
                todo.append((second, first, earlier, -1.0))
            for r, (a, b, chunks, sign) in enumerate(todo):
                total = product(a, b, chunks, sign)
                wide = total.shape[1]
                for m in range(NLAG):
                    sends[g][r][m, p, :, :wide] = total[m * new : (m + 1) * new].astype(BF16)
                    if wide < shapes[r][1]:
                        sends[g][r][m, p, :, wide:] = jnp.zeros((new, shapes[r][1] - wide), BF16)
                for d in (2, 1, 3):
                    across(g, r, d, p).start()
            return carry

        run(one_pair, low, high)

    def run(body, low, high):
        if high - low == 1:
            body(low, 0)
        else:
            lax.fori_loop(low, high, body, 0)

    def across(g, r, d, p):
        place = sum(spans[:g]) + r
        lag = (y + d) % 4
        return pltpu.make_async_remote_copy(
            src_ref=sends[g][r].at[lag, p],
            dst_ref=lands[g][r].at[d - 1, p],
            send_sem=ysem.at[place, d - 1, p],
            recv_sem=yrsem.at[place, d - 1, p],
            device_id=(h, lag),
            device_id_type=MESH,
        )

    def store(p):
        sem = in_sem.at[CHUNKS + TABLE_CUTS + 2 + p]
        return pltpu.make_async_copy(out.at[p], result.at[0, p], sem)

    def finish(g):
        new, old, shapes = regions(GROUPS[g])
        scale = 1.0 / math.sqrt(NF * SEG * 4)

        def one_pair(p, carry):
            for r in range(spans[g]):
                total = sends[g][r][y, p].astype(F32)
                for d in (1, 3, 2):
                    across(g, r, d, p).wait_recv()
                    total += lands[g][r][d - 1, p].astype(F32)
                total *= scale
                if r == 0:
                    out[p, old : old + new, : old + new] = total[:, : old + new]
                else:
                    out[p, :old, old : old + new] = total.T[:old]
                for d in (1, 2, 3):
                    across(g, r, d, p).wait_send()
            if g == len(GROUPS) - 1:
                store(p).start()
            return carry

        lax.fori_loop(0, PAIRS, one_pair, 0)

    steps = {
        "S": spectra,
        "Z": ring,
        "O": loop,
        "B": share,
        "H": ring_on,
        "I": ring_rest,
        "L": lambda t: loop_on(t, (0, 1)),
        "M": lambda t: loop_on(t, (2, 3)),
        "X": cross,
        "C": crossed,
        "E": last_hop,
        "T": settle,
        "G": finish,
    }
    at = 0
    while at < len(ORDER):
        step = ORDER[at]
        at += 1
        if step[0] == "K":
            g, low = int(step[1]), int(step[2])
            high = low + 1
            while at < len(ORDER) and ORDER[at] == step[:2] + str(high):
                high += 1
                at += 1
            correlate(g, low, high)
            step = "K" + str(g) + str(high - 1)
        else:
            steps[step[0]](int(step[1]))
        if step == LAST:
            for done in started:
                done()
        if step == "S0":
            pl.semaphore_wait(barrier, len(partners))

    for p in range(PAIRS):
        store(p).wait()


def local(traces, pairs):
    table, window, small = host_tables()
    scratch = [pltpu.VMEM((BLOCKS, SEG, size, 2 * NF), BF16) for size in SIZES]
    spans = 0
    for group in GROUPS:
        shapes = regions(group)[2]
        spans += len(shapes)
        scratch += [pltpu.VMEM((NLAG, PAIRS, *shape), BF16) for shape in shapes]
        scratch += [pltpu.VMEM((3, PAIRS, *shape), BF16) for shape in shapes]
    widest = max(regions(group)[0] for group in GROUPS)
    scratch += [
        pltpu.VMEM((CB, SEG, L), BF16),
        pltpu.VMEM((L, 2 * NF), BF16),
        pltpu.VMEM((NF, NF), BF16),
        pltpu.VMEM((8, NF), F32),
        pltpu.VMEM((2 * NF // 128, SEG * max(SIZES), 128), F32),
        pltpu.VMEM((SEG, NLAG * widest, 2 * NF), BF16),
        pltpu.VMEM((PAIRS, CB, CB), F32),
        pltpu.SemaphoreType.DMA((CHUNKS + TABLE_CUTS + 2 + PAIRS,)),
        pltpu.SemaphoreType.DMA((CHUNKS, COPIES)),
        pltpu.SemaphoreType.DMA((CHUNKS, COPIES)),
        pltpu.SemaphoreType.DMA((spans, 3, PAIRS)),
        pltpu.SemaphoreType.DMA((spans, 3, PAIRS)),
    ]
    return pl.pallas_call(
        kernel,
        out_shape=jax.ShapeDtypeStruct((1, PAIRS, CB, CB), F32),
        in_specs=[
            pl.BlockSpec(memory_space=pl.ANY),
            pl.BlockSpec(memory_space=pl.ANY),
            pl.BlockSpec(memory_space=pl.ANY),
            pl.BlockSpec(memory_space=pl.ANY),
            pl.BlockSpec(memory_space=pltpu.SMEM),
        ],
        out_specs=pl.BlockSpec(memory_space=pl.ANY),
        scratch_shapes=scratch,
        compiler_params=pltpu.CompilerParams(
            collective_id=0, has_side_effects=True, vmem_limit_bytes=62 << 20
        ),
        name="correlate_pairs",
    )(traces, jnp.asarray(table), jnp.asarray(window), jnp.asarray(small), pairs.T)


def solution(mesh):
    placed = (P("chan", "seg", None), P("chan", None))
    return jax.shard_map(
        local, mesh=mesh, in_specs=placed, out_specs=P("seg", "chan", None, None), check_vma=False
    )
```

```python
import math

import jax
import jax.numpy as jnp
import numpy as np
from jax import lax
from jax.experimental import pallas as pl
from jax.experimental.pallas import tpu as pltpu
from jax.sharding import PartitionSpec as P

CB = 256
L = 4096
NF = 512
FLO = 64
HW = 64
LAGSTEP = 16
NLAG = 4
PAIRS = 4
BLOCKS = 32
SEG = 2
SIZES = (64, 64, 64, 64)
CHUNKS = len(SIZES)
STARTS = tuple(sum(SIZES[:t]) for t in range(CHUNKS))
GROUPS = ((0, 1), (2,), (3,))
TABLE_CUTS = 4
AHEAD = 7
MESH = pl.DeviceIdType.MESH
BF16 = jnp.bfloat16
F32 = jnp.float32

ORDER = (
    "S0", "Z0", "O0", "S1", "B1", "S2", "S3", "O2", "M0", "Z1", "O3", "B2", "O1", "H0", "I0",
    "M2", "L0", "H1", "I1", "X0", "Z2", "X1", "M1", "C0", "H2", "I2", "L1", "B3", "Z3", "X2",
    "B0", "E0", "T0", "C1", "L2", "H3", "I3", "E1", "T1", "K00", "K01", "K02", "C2", "E2", "K03",
    "X3", "L3", "T2", "K10", "K11", "G0", "K12", "K13", "M3", "C3", "E3", "T3", "K20", "K21",
    "K22", "K23", "G1", "G2",
)

LAST = "K" + str(len(GROUPS) - 1) + str(PAIRS - 1)

ZP, ZM, ZA, ZB, ZC, XN, XE, ZE, LA, LB, SB = 0, 2, 4, 5, 6, 7, 9, 10, 11, 15, 19
COPIES = 25


def host_tables():
    sample = np.arange(L)
    bins = FLO + np.arange(NF)
    angles = 2.0 * np.pi / L * ((sample[:, None] * bins[None, :]) % L)
    taper = (0.5 - 0.5 * np.cos(2.0 * np.pi / L * sample))[:, None] / math.sqrt(L)
    table = np.concatenate([taper * np.cos(angles), -taper * np.sin(angles)], axis=1)
    rows = np.arange(NF)
    window = np.abs(rows[:, None] - rows[None, :]) <= HW
    phase = 2.0 * np.pi / L * ((LAGSTEP * bins) % L)
    small = np.zeros((8, NF), np.float32)
    small[0], small[1] = np.cos(phase), np.sin(phase)
    small[2], small[3] = np.cos(2.0 * phase), np.sin(2.0 * phase)
    small[4] = 1.0 / window.sum(axis=0)
    return table.astype(BF16), window.astype(BF16), small


def regions(group):
    new = sum(SIZES[t] for t in group)
    old = STARTS[group[0]]
    shapes = [(new, -(-(old + new) // 128) * 128)]
    if old:
        shapes.append((new, -(-old // 128) * 128))
    return new, old, shapes


def kernel(traces, table_hbm, window_hbm, small_hbm, pairs, result, *scratch):
    pools = scratch[:CHUNKS]
    scratch = scratch[CHUNKS:]
    spans = [len(regions(group)[2]) for group in GROUPS]
    sends, lands = [], []
    for span in spans:
        sends.append(scratch[:span])
        lands.append(scratch[span : 2 * span])
        scratch = scratch[2 * span :]
    rows_in, table, window, small, white, rot, out, in_sem, ssem, rsem, ysem, yrsem = scratch

    h = lax.axis_index("chan")
    y = lax.axis_index("seg")
    core = h % 2
    z = (h // 2) % 4
    x = h // 8
    away = 1 - 2 * (z // 2)
    outer = (z == 0) | (z == 3)
    gives = (x + away >= 0) & (x + away <= 3)
    takes = (x - away >= 0) & (x - away <= 3)

    def node(xx, zz, cc=None):
        return ((xx % 4) * 8 + (zz % 4) * 2 + (core if cc is None else cc), y)

    def slot(xx, zz, cc=None):
        return node(xx, zz, cc)[0]

    sibling = node(x, z, 1 - core)
    partners = [node(x, z + 1), node(x, z + 3), node(x + 1, z), node(x + 3, z), sibling]
    partners += [(h, (y + d) % 4) for d in (1, 2, 3)]

    fetch_rows = [
        pltpu.make_async_copy(
            traces.at[pl.ds(STARTS[t], SIZES[t])],
            rows_in.at[pl.ds(STARTS[t], SIZES[t])],
            in_sem.at[t],
        )
        for t in range(CHUNKS)
    ]
    cut = L // TABLE_CUTS
    fetch_table = [
        pltpu.make_async_copy(
            table_hbm.at[pl.ds(i * cut, cut)], table.at[pl.ds(i * cut, cut)], in_sem.at[CHUNKS + i]
        )
        for i in range(TABLE_CUTS)
    ]
    fetch_small = [
        pltpu.make_async_copy(window_hbm, window, in_sem.at[CHUNKS + TABLE_CUTS]),
        pltpu.make_async_copy(small_hbm, small, in_sem.at[CHUNKS + TABLE_CUTS + 1]),
    ]
    fetches = [fetch_rows[0], *fetch_table, *fetch_small, *fetch_rows[1:]]
    for copy in fetches[:AHEAD]:
        copy.start()

    barrier = pltpu.get_barrier_semaphore()
    for partner in partners:
        pl.semaphore_signal(barrier, inc=1, device_id=partner, device_id_type=MESH)

    def spectra(t):
        fetch_rows[t].wait()
        size = SIZES[t]
        rows = rows_in[STARTS[t] : STARTS[t] + size].reshape(SEG * size, L)
        if t == 0:
            spec = jnp.zeros((SEG * size, 2 * NF), F32)
            for i in range(TABLE_CUTS):
                fetch_table[i].wait()
                for copy in fetches[i + AHEAD : i + AHEAD + 1]:
                    copy.start()
                spec += jnp.dot(
                    rows[:, i * cut : (i + 1) * cut],
                    table[i * cut : (i + 1) * cut],
                    preferred_element_type=F32,
                )
        else:
            spec = jnp.dot(rows, table[...], preferred_element_type=F32)
        if t == 0:
            for copy in fetch_small:
                copy.wait()
        real, imag = spec[:, :NF], spec[:, NF:]
        power = real * real + imag * imag
        high = power.astype(BF16)
        low = (power - high.astype(F32)).astype(BF16)
        smooth = jnp.dot(high, window[...], preferred_element_type=F32)
        smooth += jnp.dot(low, window[...], preferred_element_type=F32)
        factor = lax.rsqrt(smooth * small[4:5, :] + 1e-06)
        for j in range(2 * NF // 128):
            part = real if j * 128 < NF else imag
            lanes = slice(j * 128 % NF, j * 128 % NF + 128)
            white[j, : SEG * size] = part[:, lanes] * factor[:, lanes]
            for s in range(SEG):
                rows = white[j, pl.ds(s, size, stride=SEG), :]
                pools[t][h, s, :, j * 128 : (j + 1) * 128] = rows.astype(BF16)

    started = []

    def remote(t, what, block, part, target):
        view = pools[t].at[(block, *part)]
        return pltpu.make_async_remote_copy(
            src_ref=view,
            dst_ref=view,
            send_sem=ssem.at[t, what],
            recv_sem=rsem.at[t, what],
            device_id=target,
            device_id_type=MESH,
        )

    def on(condition, act):
        if condition is None:
            act()
        else:
            pl.when(condition)(act)

    def send(t, what, block, part, target, condition=None):
        on(condition, lambda: remote(t, what, block, part, target).start())
        started.append(
            lambda: on(condition, lambda: remote(t, what, block, part, target).wait_send())
        )

    def take(t, what, block, part, condition=None):
        on(condition, lambda: remote(t, what, block, part, sibling).wait_recv())

    def loop_parts(t):
        size = SIZES[t]
        low = max(size // 4, 16)
        cuts = [(0,), (1, pl.ds(size // 2, size // 2))]
        if low < size // 2:
            cuts.append((1, pl.ds(low, size // 2 - low)))
        cuts.append((1, pl.ds(0, low)))
        return list(zip(cuts, loop_way))

    middle = jnp.where(outer, 1, -1)
    loop_way = [-away, -away, -away * middle, away]

    def ring(t):
        own = slot(x, z)
        send(t, ZP, own, (0,), node(x, z + 1))
        send(t, ZM + 1, own, (1,), node(x, z + 3))
        send(t, ZP + 1, own, (1,), node(x, z + 1), z != 3)
        send(t, ZM, own, (0,), node(x, z + 3), z != 0)

    def loop(t):
        for i, (part, way) in enumerate(loop_parts(t)):
            send(t, LA + i, slot(x, z), part, node(x + way + 4, z))

    def share(t):
        send(t, SB, slot(x, z), (), sibling)

    def ring_on(t):
        below, above = slot(x, z + 3), slot(x, z + 1)
        take(t, ZP, below, (0,))
        send(t, ZA, below, (0,), node(x, z + 1), z != 2)
        take(t, ZM + 1, above, (1,))
        send(t, ZB, above, (1,), node(x, z + 3), z != 1)

    def ring_rest(t):
        below, above = slot(x, z + 3), slot(x, z + 1)
        take(t, ZP + 1, below, (1,), z != 0)
        take(t, ZM, above, (0,), z != 3)
        side = z // 3
        send(t, ZC, slot(x, z + 1 + 2 * side), (side,), node(x, z + 3 + 2 * side), outer)
        send(t, XE, slot(x, 3 - z), (side,), node(x + away + 4, z), outer & gives)
        send(t, SB + 1, below, (), sibling, z != 0)
        send(t, SB + 2, above, (), sibling, z != 3)

    def loop_on(t, which):
        for i, (part, way) in enumerate(loop_parts(t)):
            if i in which:
                block = slot(x - way + 4, z)
                take(t, LA + i, block, part)
                send(t, LB + i, block, part, node(x + way + 4, z))

    def cross(t):
        far = slot(x, z + 2)
        side = z // 3
        on(z != 3, lambda: remote(t, ZA, far, (0,), sibling).wait_recv())
        on(z != 0, lambda: remote(t, ZB, far, (1,), sibling).wait_recv())
        on(outer, lambda: remote(t, ZC, far, (1 - side,), sibling).wait_recv())
        for s in range(SEG):
            send(t, XN + s, far, (s,), node(x + away + 4, z), gives)
        send(t, SB + 3, far, (), sibling, core == z // 2)

    def crossed(t):
        near = slot(x - away + 4, z + 2)
        for s in range(SEG):
            take(t, XN + s, near, (s,), takes)
        inner = jnp.logical_not(outer)
        send(t, ZE, near, (jnp.clip(2 - z, 0, 1),), node(x, 3 * (z // 2)), inner & takes)
        send(t, SB + 4, near, (), sibling, takes & (core == 1 - z // 2))

    def last_hop(t):
        edge = slot(x - away + 4, 3 - z)
        side = z // 3
        take(t, XE, edge, (side,), outer & takes)
        take(t, ZE, edge, (1 - side,), outer & takes)
        send(t, SB + 5, edge, (), sibling, outer & takes)

    def settle(t):
        other = 1 - core
        for i, (part, _) in enumerate(loop_parts(t)):
            take(t, LB + i, slot(x + 2, z), part)
        take(t, SB, slot(x, z, other), ())
        take(t, SB + 1, slot(x, z + 3, other), (), z != 0)
        take(t, SB + 2, slot(x, z + 1, other), (), z != 3)
        take(t, SB + 3, slot(x, z + 2, other), (), other == z // 2)
        take(t, SB + 4, slot(x - away + 4, z + 2, other), (), takes & (other == 1 - z // 2))
        take(t, SB + 5, slot(x - away + 4, 3 - z, other), (), outer & takes)

    def rotate(block, sign):
        real, imag = block[:, :NF].astype(F32), block[:, NF:].astype(F32)
        cos1, sin1 = small[0:1, :], small[1:2, :] * sign
        cos2, sin2 = small[2:3, :], small[3:4, :] * sign
        rc, ic, rs, js = real * cos1, imag * cos1, real * sin1, imag * sin1
        back2 = (real * cos2 + imag * sin2, imag * cos2 - real * sin2)
        back1 = (rc + js, ic - rs)
        ahead = (rc - js, ic + rs)
        return back2, back1, None, ahead

    def gather_rows(block, s, chunks):
        parts = [pools[t][block, s] for t in chunks]
        return parts[0] if len(parts) == 1 else jnp.concatenate(parts, axis=0)

    def correlate(g, low, high):
        group = GROUPS[g]
        new, old, shapes = regions(group)
        earlier = tuple(range(group[0]))

        def product(first, second, chunks, sign):
            total = None
            for s in range(SEG):
                for t in group:
                    block = pools[t][first, s]
                    for m, turned in enumerate(rotate(block, sign)):
                        at = m * new + STARTS[t] - old
                        end = at + SIZES[t]
                        if turned is None:
                            rot[s, at:end] = block
                        else:
                            rot[s, at:end, :NF] = turned[0].astype(BF16)
                            rot[s, at:end, NF:] = turned[1].astype(BF16)
                term = lax.dot_general(
                    rot[s, : NLAG * new],
                    gather_rows(second, s, chunks),
                    (((1,), (1,)), ((), ())),
                    preferred_element_type=F32,
                )
                total = term if total is None else total + term
            return total

        def one_pair(p, carry):
            first, second = pairs[0, p], pairs[1, p]
            todo = [(first, second, earlier + group, 1.0)]
            if old:
                todo.append((second, first, earlier, -1.0))
            for r, (a, b, chunks, sign) in enumerate(todo):
                total = product(a, b, chunks, sign)
                wide = total.shape[1]
                for m in range(NLAG):
                    sends[g][r][m, p, :, :wide] = total[m * new : (m + 1) * new].astype(BF16)
                    if wide < shapes[r][1]:
                        sends[g][r][m, p, :, wide:] = jnp.zeros((new, shapes[r][1] - wide), BF16)
                for d in (2, 1, 3):
                    across(g, r, d, p).start()
            return carry

        run(one_pair, low, high)

    def run(body, low, high):
        if high - low == 1:
            body(low, 0)
        else:
            lax.fori_loop(low, high, body, 0)

    def across(g, r, d, p):
        place = sum(spans[:g]) + r
        lag = (y + d) % 4
        return pltpu.make_async_remote_copy(
            src_ref=sends[g][r].at[lag, p],
            dst_ref=lands[g][r].at[d - 1, p],
            send_sem=ysem.at[place, d - 1, p],
            recv_sem=yrsem.at[place, d - 1, p],
            device_id=(h, lag),
            device_id_type=MESH,
        )

    def store(p):
        sem = in_sem.at[CHUNKS + TABLE_CUTS + 2 + p]
        return pltpu.make_async_copy(out.at[p], result.at[0, p], sem)

    def finish(g):
        new, old, shapes = regions(GROUPS[g])
        scale = 1.0 / math.sqrt(NF * SEG * 4)

        def one_pair(p, carry):
            for r in range(spans[g]):
                total = sends[g][r][y, p].astype(F32)
                for d in (1, 3, 2):
                    across(g, r, d, p).wait_recv()
                    total += lands[g][r][d - 1, p].astype(F32)
                total *= scale
                if r == 0:
                    out[p, old : old + new, : old + new] = total[:, : old + new]
                else:
                    out[p, :old, old : old + new] = total.T[:old]
                for d in (1, 2, 3):
                    across(g, r, d, p).wait_send()
            if g == len(GROUPS) - 1:
                store(p).start()
            return carry

        lax.fori_loop(0, PAIRS, one_pair, 0)

    steps = {
        "S": spectra,
        "Z": ring,
        "O": loop,
        "B": share,
        "H": ring_on,
        "I": ring_rest,
        "L": lambda t: loop_on(t, (0, 1)),
        "M": lambda t: loop_on(t, (2, 3)),
        "X": cross,
        "C": crossed,
        "E": last_hop,
        "T": settle,
        "G": finish,
    }
    at = 0
    while at < len(ORDER):
        step = ORDER[at]
        at += 1
        if step[0] == "K":
            g, low = int(step[1]), int(step[2])
            high = low + 1
            while at < len(ORDER) and ORDER[at] == step[:2] + str(high):
                high += 1
                at += 1
            correlate(g, low, high)
            step = "K" + str(g) + str(high - 1)
        else:
            steps[step[0]](int(step[1]))
        if step == LAST:
            for done in started:
                done()
        if step == "S0":
            pl.semaphore_wait(barrier, len(partners))

    for p in range(PAIRS):
        store(p).wait()


def local(traces, pairs):
    table, window, small = host_tables()
    scratch = [pltpu.VMEM((BLOCKS, SEG, size, 2 * NF), BF16) for size in SIZES]
    spans = 0
    for group in GROUPS:
        shapes = regions(group)[2]
        spans += len(shapes)
        scratch += [pltpu.VMEM((NLAG, PAIRS, *shape), BF16) for shape in shapes]
        scratch += [pltpu.VMEM((3, PAIRS, *shape), BF16) for shape in shapes]
    widest = max(regions(group)[0] for group in GROUPS)
    scratch += [
        pltpu.VMEM((CB, SEG, L), BF16),
        pltpu.VMEM((L, 2 * NF), BF16),
        pltpu.VMEM((NF, NF), BF16),
        pltpu.VMEM((8, NF), F32),
        pltpu.VMEM((2 * NF // 128, SEG * max(SIZES), 128), F32),
        pltpu.VMEM((SEG, NLAG * widest, 2 * NF), BF16),
        pltpu.VMEM((PAIRS, CB, CB), F32),
        pltpu.SemaphoreType.DMA((CHUNKS + TABLE_CUTS + 2 + PAIRS,)),
        pltpu.SemaphoreType.DMA((CHUNKS, COPIES)),
        pltpu.SemaphoreType.DMA((CHUNKS, COPIES)),
        pltpu.SemaphoreType.DMA((spans, 3, PAIRS)),
        pltpu.SemaphoreType.DMA((spans, 3, PAIRS)),
    ]
    return pl.pallas_call(
        kernel,
        out_shape=jax.ShapeDtypeStruct((1, PAIRS, CB, CB), F32),
        in_specs=[
            pl.BlockSpec(memory_space=pl.ANY),
            pl.BlockSpec(memory_space=pl.ANY),
            pl.BlockSpec(memory_space=pl.ANY),
            pl.BlockSpec(memory_space=pl.ANY),
            pl.BlockSpec(memory_space=pltpu.SMEM),
        ],
        out_specs=pl.BlockSpec(memory_space=pl.ANY),
        scratch_shapes=scratch,
        compiler_params=pltpu.CompilerParams(
            collective_id=0, has_side_effects=True, vmem_limit_bytes=62 << 20
        ),
        name="correlate_pairs",
    )(traces, jnp.asarray(table), jnp.asarray(window), jnp.asarray(small), pairs.T)


def solution(mesh):
    placed = (P("chan", "seg", None), P("chan", None))
    return jax.shard_map(
        local, mesh=mesh, in_specs=placed, out_specs=P("seg", "chan", None, None), check_vma=False
    )
```
